256 devices in a mesh: group: 8 (over x_lo, y), fsdp: 32 (over z, x_hi, core).
Axes of the slice: x: 4 (x_hi: 2, x_lo: 2; x = x_hi * 2 + x_lo), y: 4, z: 8, core: 2. Of those that a mesh axis runs over, the one named last changes fastest.
Arguments:
- cotangent: bfloat16 [8, 4096, 1536], P('group', 'fsdp'), may hold values from -6 to 6
- down_weight: bfloat16 [8, 12288, 1536], P('group', 'fsdp'), may hold values from -0.0546875 to 0.0546875
- gate_weight: bfloat16 [8, 1536, 12288], P('group', None, 'fsdp'), may hold values from -0.15625 to 0.15625
- up_weight: bfloat16 [8, 1536, 12288], P('group', None, 'fsdp'), may hold values from -0.15625 to 0.15625
- preacts: bfloat16 [8, 2, 4096, 12288], P('group', None, None, 'fsdp'), may hold values from -6 to 6
- pseudo_grad: float32 [8, 1572864], P('group', 'fsdp'), may hold values from -6 to 6
- first_moment: float32 [8, 1572864], P('group', 'fsdp'), may hold values from -4 to 4
- second_moment: float32 [8, 1572864], P('group', 'fsdp'), may hold values from 0.1 to 4
Outputs:
- input_grad: bfloat16 [8, 4096, 1536], P('group', 'fsdp')
- fragment_mean: float32 [3, 1572864], P(None, 'fsdp')
The draws below stay inside these ranges and needn't reach their ends.
All inputs are finite; a program needn't handle non-finite values.
Results may differ from the reference program's by a relative error of at most 0.02.
Values may be sent and summed in bfloat16 or wider, within the bound.
No kernel may reach another device: no remote copies, remote signals or barrier semaphores. Data moves between devices by JAX's collectives and lax.ppermute only.
A program may use at most 128 MiB of HBM per device.

```python
import math
import jax
import jax.numpy as jnp
from jax import lax

D = 1536
FF = 12288
TOKENS = 4096
FRAG = 1572864
N_GROUP = 8
N_FSDP = 32


def level_of(key, extent, shards, low, high):
    gain, own = 1.0, jax.random.fold_in(key, 6)
    for dim, shards_of in shards:
        heights = jnp.exp(jax.random.uniform(jax.random.fold_in(own, dim), (shards_of,), jnp.float32, low / len(shards), high / len(shards)))
        gain = gain * jnp.repeat(heights, extent[dim] // shards_of).reshape([-1 if axis == dim else 1 for axis in range(len(extent))])
    return gain


def scatter_about(key, shape, deviation, most, split=(), kind=jnp.bfloat16):
    drawn = jax.random.normal(key, shape, jnp.float32) * deviation
    if len(split) > 0:
        drawn = level_of(key, shape, split, -0.22, 0.18) * drawn
    return jnp.clip(drawn, min=-most, max=most).astype(kind)


def setup_inputs(seed: int = 0) -> dict:
    keys = jax.random.split(jax.random.key(seed), 9)
    return {
        "cotangent": scatter_about(keys[0], (N_GROUP, TOKENS, D), 1.0, 6.0, ((0, 8), (1, 32))),
        "down_weight": scatter_about(keys[1], (N_GROUP, FF, D), FF ** -0.5, 0.0546875, ((0, 8), (1, 32))),
        "gate_weight": scatter_about(keys[2], (N_GROUP, D, FF), D ** -0.5, 0.15625, ((0, 8), (2, 32))),
        "up_weight": scatter_about(keys[3], (N_GROUP, D, FF), D ** -0.5, 0.15625, ((0, 8), (2, 32))),
        "preacts": scatter_about(keys[4], (N_GROUP, 2, TOKENS, FF), 1.0, 6.0, ((0, 8), (3, 32))),
        "pseudo_grad": scatter_about(keys[5], (N_GROUP, FRAG), 1.0, 6.0, ((0, 8), (1, 32)), jnp.float32),
        "first_moment": scatter_about(keys[6], (N_GROUP, FRAG), 0.5, 4.0, ((0, 8), (1, 32)), jnp.float32),
        "second_moment": jnp.clip(jnp.exp(math.log(4.0) - 3.6888794 * jax.random.uniform(keys[7], (N_GROUP, FRAG), jnp.float32) ** level_of(keys[7], (N_GROUP, FRAG), ((0, 8), (1, 32)), -0.2, 0.2)), 0.1, 4.0),
    }


tanh_scale = math.sqrt(2.0 / math.pi)
cubic_coef = 0.044715

def gelu_parts(preact):
    tanh_part = jnp.tanh(tanh_scale * (preact + cubic_coef * preact * preact * preact))
    activated = 0.5 * preact * (1.0 + tanh_part)
    derivative = 0.5 * (1.0 + tanh_part) + 0.5 * preact * (1.0 - tanh_part * tanh_part) * tanh_scale * (1.0 + 3.0 * cubic_coef * preact * preact)
    return (activated, derivative)

def one_group(inputs):
    cotangent, down_weight, gate_weight, up_weight, preacts = inputs
    hidden_width = FF // N_FSDP

    def shard_term(running, position):
        offset = (position * hidden_width).astype(jnp.int32)
        down_rows = lax.dynamic_slice_in_dim(down_weight, offset, hidden_width, 0)
        gate_cols = lax.dynamic_slice_in_dim(gate_weight, offset, hidden_width, 1)
        up_cols = lax.dynamic_slice_in_dim(up_weight, offset, hidden_width, 1)
        gate_pre = lax.dynamic_slice_in_dim(preacts[0], offset, hidden_width, 1).astype(jnp.float32)
        up_pre = lax.dynamic_slice_in_dim(preacts[1], offset, hidden_width, 1).astype(jnp.float32)
        hidden_grad = jnp.dot(cotangent, down_rows.T, preferred_element_type=jnp.float32)
        activated, derivative = gelu_parts(gate_pre)
        gate_grad = (hidden_grad * up_pre * derivative).astype(jnp.bfloat16)
        up_grad = (hidden_grad * activated).astype(jnp.bfloat16)
        partial_sum = jnp.dot(gate_grad, gate_cols.T, preferred_element_type=jnp.float32) + jnp.dot(up_grad, up_cols.T, preferred_element_type=jnp.float32)
        rounded = lax.optimization_barrier(partial_sum.astype(jnp.bfloat16)).astype(jnp.float32)
        return (running + rounded, None)
    start_sum = jnp.zeros((cotangent.shape[0], cotangent.shape[1]), jnp.float32)
    running, _ = lax.scan(shard_term, start_sum, jnp.arange(N_FSDP, dtype=jnp.int32))
    return running.astype(jnp.bfloat16)

def reference(cotangent, down_weight, gate_weight, up_weight, preacts, pseudo_grad, first_moment, second_moment):
    input_grad = lax.map(one_group, (cotangent, down_weight, gate_weight, up_weight, preacts))
    fragment_mean = jnp.stack([lax.optimization_barrier(jnp.sum(pseudo_grad, axis=0)) / N_GROUP, lax.optimization_barrier(jnp.sum(first_moment, axis=0)) / N_GROUP, lax.optimization_barrier(jnp.sum(second_moment, axis=0)) / N_GROUP])
    return (input_grad, fragment_mean)
```

```python
import functools
import math

import jax
import jax.numpy as jnp
from jax import lax
from jax.experimental import pallas as pl
from jax.experimental.pallas import tpu as pltpu
from jax.sharding import PartitionSpec as P

tanh_scale = math.sqrt(2.0 / math.pi)
cubic_coef = 0.044715

Z, XH, CORE = 8, 2, 2
ROWS = 128
HALF = ROWS // 2
D = 1536
HID = 384
BLOCK = 256
VMEM_BYTES = 60 * 1024 * 1024


def device_of(z, xh, core):
    return ((z % Z) * XH + xh) * CORE + core


def moves(where):
    return [
        (device_of(z, xh, core), device_of(*where(z, xh, core)))
        for z in range(Z)
        for xh in range(XH)
        for core in range(CORE)
    ]


def along_z(value, step):
    return lax.ppermute(value, "fsdp", moves(lambda z, xh, core: (z + step, xh, core)))


def across_x(value):
    return lax.ppermute(value, "fsdp", moves(lambda z, xh, core: (z, 1 - xh, core)))


def to_sibling(value):
    return lax.ppermute(value, "fsdp", moves(lambda z, xh, core: (z, xh, 1 - core)))


def contract_last(left, right):
    return lax.dot_general(left, right, (((1,), (1,)), ((), ())), preferred_element_type=jnp.float32)


def grads_kernel(units, deps, index, *refs):
    cot = refs[:units]
    preacts = refs[units : units + 2]
    weights = refs[units + 2 : units + 8]
    same_ref, cross_ref, rows_ref, pre_ref, down_ref, mixed_ref, grads_ref, sems = refs[units + 8 + deps :]

    def load(source, target, sem):
        copy = pltpu.make_async_copy(source, target, sems.at[sem])
        copy.start()
        return copy

    first = []
    for i in range(units):
        first.append(load(cot[i], rows_ref.at[pl.ds(i * ROWS, ROWS), :], i))
    for i in range(2):
        first.append(load(weights[i], down_ref.at[pl.ds(i * HID, HID), :], units + i))
    for i in range(units):
        source = pl.ds(pl.multiple_of(index[i] * ROWS, ROWS), ROWS)
        for j in range(2):
            target = pre_ref.at[:, pl.ds(i * ROWS, ROWS), pl.ds(j * HID, HID)]
            first.append(load(preacts[j].at[:, source, :], target, units + 2 + 2 * i + j))
    second = []
    for i in range(4):
        target = mixed_ref.at[:, pl.ds(i * HID, HID)]
        second.append(load(weights[2 + i], target, 3 * units + 2 + i))
    for copy in first:
        copy.wait()
    for block in range(3):
        left = block * BLOCK
        hidden = contract_last(rows_ref[...], down_ref[left : left + BLOCK, :])
        for i in range(units):
            rows = slice(i * ROWS, (i + 1) * ROWS)
            gate = pre_ref[0, rows, left : left + BLOCK].astype(jnp.float32)
            up = pre_ref[1, rows, left : left + BLOCK].astype(jnp.float32)
            square = gate * gate
            tanh_part = jnp.tanh(gate * (tanh_scale + (tanh_scale * cubic_coef) * square))
            share = 0.5 + 0.5 * tanh_part
            activated = gate * share
            derivative = share + activated * (1.0 - share) * (
                2.0 * tanh_scale + (6.0 * tanh_scale * cubic_coef) * square
            )
            part = hidden[rows, :]
            grads_ref[rows, left : left + BLOCK] = (part * up * derivative).astype(jnp.bfloat16)
            right = left + 2 * HID
            grads_ref[rows, right : right + BLOCK] = (part * activated).astype(jnp.bfloat16)
    for copy in second:
        copy.wait()
    half = units // 2 * ROWS

    def column_block(step, carry):
        columns = pl.ds(pl.multiple_of(step * BLOCK, BLOCK), BLOCK)
        partial = contract_last(grads_ref[...], mixed_ref[columns, :]).astype(jnp.bfloat16)
        same_ref[:, columns] = partial[:half]
        cross_ref[:, columns] = partial[half:]
        return carry

    lax.fori_loop(0, D // BLOCK, column_block, 0)


ANYWHERE = pl.BlockSpec(memory_space=pl.ANY)


def chunk_partials(cot, index, preacts, weights, deps=()):
    units = len(cot)
    rows, half = units * ROWS, units // 2 * ROWS
    result = pl.BlockSpec((half, D), lambda _, index: (0, 0))
    return pl.pallas_call(
        functools.partial(grads_kernel, units, len(deps)),
        grid_spec=pltpu.PrefetchScalarGridSpec(
            num_scalar_prefetch=1,
            grid=(1,),
            in_specs=[ANYWHERE] * (units + 8 + len(deps)),
            out_specs=[result, result],
            scratch_shapes=[
                pltpu.VMEM((rows, D), jnp.bfloat16),
                pltpu.VMEM((2, rows, 2 * HID), jnp.bfloat16),
                pltpu.VMEM((2 * HID, D), jnp.bfloat16),
                pltpu.VMEM((D, 4 * HID), jnp.bfloat16),
                pltpu.VMEM((rows, 4 * HID), jnp.bfloat16),
                pltpu.SemaphoreType.DMA((3 * units + 6,)),
            ],
        ),
        out_shape=[jax.ShapeDtypeStruct((half, D), jnp.bfloat16)] * 2,
        cost_estimate=pl.CostEstimate(
            flops=rows * 6 * D * 2 * HID,
            bytes_accessed=12 * D * HID + rows * (4 * D + 8 * HID),
            transcendentals=rows * 2 * HID,
        ),
        compiler_params=pltpu.CompilerParams(vmem_limit_bytes=VMEM_BYTES),
    )(index, *cot, *preacts, *weights, *deps)


def pass_on(*refs):
    pass


def after(values, first):
    return pl.pallas_call(
        pass_on,
        in_specs=[ANYWHERE] * (len(values) + len(first)),
        out_specs=[ANYWHERE] * len(values),
        out_shape=[jax.ShapeDtypeStruct(value.shape, value.dtype) for value in values],
        input_output_aliases={i: i for i in range(len(values))},
        compiler_params=pltpu.CompilerParams(vmem_limit_bytes=VMEM_BYTES),
    )(*values, *first)


def add(*terms):
    total = terms[0].astype(jnp.float32)
    for term in terms[1:]:
        total = total + term.astype(jnp.float32)
    return total.astype(jnp.bfloat16)


def local(
    cotangent,
    down_weight,
    gate_weight,
    up_weight,
    preacts,
    pseudo_grad,
    first_moment,
    second_moment,
):
    groups = lax.axis_size("group")
    place = lax.axis_index("fsdp")
    core = place % CORE
    xh = (place // CORE) % XH
    z = place // (CORE * XH)

    a, b = {0: cotangent[0]}, {}
    b[0] = across_x(a[0])
    a[-1], a[1] = along_z(a[0], 1), along_z(a[0], -1)

    own = [down_weight[0], gate_weight[0], up_weight[0]]
    weights = [weight for mine in own for weight in (mine, to_sibling(mine))]
    both_preacts = [preacts[0], to_sibling(preacts[0])]

    def partials(ks, deps=()):
        places = [((z + k) % Z) * XH + line for line in (xh, 1 - xh) for k in ks]
        index = jnp.stack([where * CORE + core for where in places]).astype(jnp.int32)
        cot = [a[k] for k in ks] + [b[k] for k in ks]
        return chunk_partials(cot, index, both_preacts, weights, deps)

    same, partners = {}, {}
    b[-1], b[1] = along_z(b[0], 1), along_z(b[0], -1)
    same[0], cross = partials((0,))
    partners[0] = across_x(cross)
    for k in (1, 2):
        a[-k], a[k] = after([a[-k], a[k]], [same[k - 1]])
        a[-k - 1], a[k + 1] = along_z(a[-k], 1), along_z(a[k], -1)
        b[-k], b[k] = after([b[-k], b[k]], [a[-k], same[k - 1]])
        b[-k - 1], b[k + 1] = along_z(b[-k], 1), along_z(b[k], -1)
        same[k], cross = partials((k, -k), [partners[k - 2]] if k > 1 else ())
        partners[k] = across_x(cross)
    a[-3], b[3] = after([a[-3], b[3]], [same[2]])
    a[4], b[4] = along_z(a[-3], 1), along_z(b[3], -1)
    same[3], cross = partials((3, -3), [partners[1]])
    partners[3] = across_x(cross)
    same[4], cross = partials((4,), [same[3], partners[2]])
    partners[4] = across_x(cross)

    parts = jnp.concatenate(
        [part.astype(jnp.bfloat16) for part in (pseudo_grad, first_moment, second_moment)], axis=0
    )
    size = groups // 2
    along_y = [
        lax.ppermute(
            parts,
            "group",
            [(x * size + y, x * size + (y + step) % size) for x in range(2) for y in range(size)],
        )
        for step in (1, 2, 3)
    ]
    line = add(parts, *along_y)
    neighbour = lax.ppermute(line, "group", [(i, (i + size) % groups) for i in range(groups)])
    fragment = (line.astype(jnp.float32) + neighbour.astype(jnp.float32)) / groups

    def terms(k, rows):
        first = 0 if k >= 0 else ROWS
        rows = slice(first + rows.start, first + rows.stop)
        return [same[abs(k)][rows], partners[abs(k)][rows]]

    sums = []
    for rows, far in ((slice(0, HALF), 1), (slice(HALF, ROWS), -1)):
        total = terms(0, rows)
        for sign in (1, -1):
            running = None
            for k in range(4 if sign == far else 3, 0, -1):
                now = terms(4 if k == 4 else sign * k, rows)
                running = along_z(add(*now, *([] if running is None else [running])), sign)
            total.append(running)
        sums.append(add(*total))
    return (jnp.concatenate(sums)[None], fragment)


def solution(mesh):
    return jax.shard_map(
        local,
        mesh=mesh,
        in_specs=(
            P("group", "fsdp", None),
            P("group", "fsdp", None),
            P("group", None, "fsdp"),
            P("group", None, "fsdp"),
            P("group", None, None, "fsdp"),
            P("group", "fsdp"),
            P("group", "fsdp"),
            P("group", "fsdp"),
        ),
        out_specs=(P("group", "fsdp", None), P(None, "fsdp")),
        check_vma=False,
    )
```

```python
import functools
import math

import jax
import jax.numpy as jnp
from jax import lax
from jax.experimental import pallas as pl
from jax.experimental.pallas import tpu as pltpu
from jax.sharding import PartitionSpec as P

tanh_scale = math.sqrt(2.0 / math.pi)
cubic_coef = 0.044715

Z, XH, CORE = 8, 2, 2
ROWS = 128
HALF = ROWS // 2
D = 1536
HID = 384
BLOCK = 256
VMEM_BYTES = 24 * 1024 * 1024


def device_of(z, xh, core):
    return ((z % Z) * XH + xh) * CORE + core


def moves(where):
    return [
        (device_of(z, xh, core), device_of(*where(z, xh, core)))
        for z in range(Z)
        for xh in range(XH)
        for core in range(CORE)
    ]


def along_z(value, step):
    return lax.ppermute(value, "fsdp", moves(lambda z, xh, core: (z + step, xh, core)))


def across_x(value):
    return lax.ppermute(value, "fsdp", moves(lambda z, xh, core: (z, 1 - xh, core)))


def to_sibling(value):
    return lax.ppermute(value, "fsdp", moves(lambda z, xh, core: (z, xh, 1 - core)))


def contract_last(left, right):
    return lax.dot_general(left, right, (((1,), (1,)), ((), ())), preferred_element_type=jnp.float32)


ANYWHERE = pl.BlockSpec(memory_space=pl.ANY)
IN_HBM = pl.BlockSpec(memory_space=pltpu.HBM)
ON_CHIP = pl.BlockSpec(memory_space=pltpu.VMEM)
PARAMS = pltpu.CompilerParams(vmem_limit_bytes=VMEM_BYTES)


def move_all(pairs, sems):
    copies = [pltpu.make_async_copy(*pair, sems.at[i]) for i, pair in enumerate(pairs)]
    for copy in copies:
        copy.start()
    return copies


def pack_kernel(down, up, _, packed, sems):
    pairs = [(up, packed.at[pl.ds(0, D), :])]
    for i in range(D // HID):
        pairs.append((down.at[:, pl.ds(i * HID, HID)], packed.at[pl.ds(D + i * HID, HID), :]))
    for copy in move_all(pairs, sems):
        copy.wait()


def pack(down, up, first):
    return pl.pallas_call(
        pack_kernel,
        in_specs=[IN_HBM, IN_HBM, ANYWHERE],
        out_specs=IN_HBM,
        out_shape=jax.ShapeDtypeStruct((2 * D, HID), jnp.bfloat16),
        scratch_shapes=[pltpu.SemaphoreType.DMA((1 + D // HID,))],
        cost_estimate=pl.CostEstimate(flops=0, bytes_accessed=0, transcendentals=0),
        compiler_params=PARAMS,
    )(down, up, first)


def join_kernel(down, gate, up, gate_other, packed, down_both, mixed, sems):
    pairs = [
        (down, down_both.at[pl.ds(0, HID), :]),
        (gate, mixed.at[:, pl.ds(0, HID)]),
        (gate_other, mixed.at[:, pl.ds(HID, HID)]),
        (up, mixed.at[:, pl.ds(2 * HID, HID)]),
        (packed.at[pl.ds(0, D), :], mixed.at[:, pl.ds(3 * HID, HID)]),
    ]
    for i in range(D // HID):
        columns = pl.ds(i * HID, HID)
        pairs.append((packed.at[pl.ds(D + i * HID, HID), :], down_both.at[pl.ds(HID, HID), columns]))
    for copy in move_all(pairs, sems):
        copy.wait()


def join(down, gate, up, gate_other, packed):
    return pl.pallas_call(
        join_kernel,
        in_specs=[IN_HBM] * 3 + [ANYWHERE] * 2,
        out_specs=[ON_CHIP] * 2,
        out_shape=[
            jax.ShapeDtypeStruct((2 * HID, D), jnp.bfloat16),
            jax.ShapeDtypeStruct((D, 4 * HID), jnp.bfloat16),
        ],
        scratch_shapes=[pltpu.SemaphoreType.DMA((5 + D // HID,))],
        cost_estimate=pl.CostEstimate(flops=0, bytes_accessed=0, transcendentals=0),
        compiler_params=PARAMS,
    )(down, gate, up, gate_other, packed)


def grads_kernel(groups, deps, *refs):
    chunks = [chunk for group in groups for chunk in group]
    units = len(chunks)
    cot = refs[:units]
    preacts = refs[units : units + 2]
    down_ref, mixed_ref = refs[units + 2 : units + 4]
    *out_refs, rows_ref, pre_ref, grads_ref, sems = refs[units + 4 + deps :]
    place = lax.axis_index("fsdp")
    core = lax.rem(place, CORE)
    xh = lax.rem(lax.div(place, CORE), XH)
    z = lax.div(place, CORE * XH)
    pairs = []
    for i, (other, k) in enumerate(chunks):
        line = 1 - xh if other else xh
        index = (lax.rem(z + k + Z, Z) * XH + line) * CORE + core
        source = pl.ds(pl.multiple_of(index * ROWS, ROWS), ROWS)
        for j in range(2):
            target = pre_ref.at[:, pl.ds(i * ROWS, ROWS), pl.ds(j * HID, HID)]
            pairs.append((preacts[j].at[:, source, :], target))
    copies = move_all(pairs, sems)
    for i in range(units):
        rows_ref[i * ROWS : (i + 1) * ROWS, :] = cot[i][...]
    for block in range(3):
        left = block * BLOCK
        hidden = contract_last(rows_ref[...], down_ref[left : left + BLOCK, :])
        if block == 0:
            for copy in copies:
                copy.wait()
        for i in range(units):
            rows = slice(i * ROWS, (i + 1) * ROWS)
            gate = pre_ref[0, rows, left : left + BLOCK].astype(jnp.float32)
            up = pre_ref[1, rows, left : left + BLOCK].astype(jnp.float32)
            square = gate * gate
            tanh_part = jnp.tanh(gate * (tanh_scale + (tanh_scale * cubic_coef) * square))
            share = 0.5 + 0.5 * tanh_part
            activated = gate * share
            derivative = share + activated * (1.0 - share) * (
                2.0 * tanh_scale + (6.0 * tanh_scale * cubic_coef) * square
            )
            part = hidden[rows, :]
            grads_ref[rows, left : left + BLOCK] = (part * up * derivative).astype(jnp.bfloat16)
            right = left + 2 * HID
            grads_ref[rows, right : right + BLOCK] = (part * activated).astype(jnp.bfloat16)

    def column_block(step, carry):
        columns = pl.ds(pl.multiple_of(step * BLOCK, BLOCK), BLOCK)
        partial = contract_last(grads_ref[...], mixed_ref[columns, :]).astype(jnp.bfloat16)
        first = 0
        for out_ref in out_refs:
            out_ref[:, columns] = partial[first : first + out_ref.shape[0]]
            first += out_ref.shape[0]
        return carry

    lax.fori_loop(0, D // BLOCK, column_block, 0)


def chunk_partials(cots, groups, preacts, weights, deps=()):
    cot = [cots[other][k] for group in groups for other, k in group]
    units = len(cot)
    rows = units * ROWS
    return pl.pallas_call(
        functools.partial(grads_kernel, groups, len(deps)),
        in_specs=[ON_CHIP] * units + [ANYWHERE] * 2 + [ON_CHIP] * 2 + [ANYWHERE] * len(deps),
        out_specs=[ON_CHIP] * len(groups),
        scratch_shapes=[
            pltpu.VMEM((rows, D), jnp.bfloat16),
            pltpu.VMEM((2, rows, 2 * HID), jnp.bfloat16),
            pltpu.VMEM((rows, 4 * HID), jnp.bfloat16),
            pltpu.SemaphoreType.DMA((2 * units,)),
        ],
        out_shape=[jax.ShapeDtypeStruct((len(group) * ROWS, D), jnp.bfloat16) for group in groups],
        cost_estimate=pl.CostEstimate(
            flops=0,
            bytes_accessed=0,
            transcendentals=0,
        ),
        compiler_params=PARAMS,
    )(*cot, *preacts, *weights, *deps)


def sums_kernel(plan, size, arrays, deps, *refs):
    out_refs = refs[arrays + deps :]
    for out_ref, terms in zip(out_refs, plan):
        total = None
        for array, first in terms:
            term = refs[array][first : first + size, :].astype(jnp.float32)
            total = term if total is None else total + term
        out_ref[...] = total.astype(jnp.bfloat16)


def row_sums(size, plan, deps=()):
    arrays = []
    places = []
    for terms in plan:
        places.append([])
        for array, first in terms:
            if not any(array is known for known in arrays):
                arrays.append(array)
            place = [array is known for known in arrays].index(True)
            places[-1].append((place, first))
    return pl.pallas_call(
        functools.partial(sums_kernel, places, size, len(arrays), len(deps)),
        in_specs=[ON_CHIP] * len(arrays) + [ANYWHERE] * len(deps),
        out_specs=[ON_CHIP] * len(plan),
        out_shape=[jax.ShapeDtypeStruct((size, D), jnp.bfloat16)] * len(plan),
        compiler_params=PARAMS,
    )(*arrays, *deps)


def pass_on(*refs):
    pass


def after(values, first):
    return pl.pallas_call(
        pass_on,
        in_specs=[ANYWHERE] * (len(values) + len(first)),
        out_specs=[ANYWHERE] * len(values),
        out_shape=[jax.ShapeDtypeStruct(value.shape, value.dtype) for value in values],
        input_output_aliases={i: i for i in range(len(values))},
        compiler_params=PARAMS,
    )(*values, *first)


def add(*terms):
    total = terms[0].astype(jnp.float32)
    for term in terms[1:]:
        total = total + term.astype(jnp.float32)
    return total.astype(jnp.bfloat16)


def add(*terms):
    total = terms[0].astype(jnp.float32)
    for term in terms[1:]:
        total = total + term.astype(jnp.float32)
    return total.astype(jnp.bfloat16)


def local(
    cotangent,
    down_weight,
    gate_weight,
    up_weight,
    preacts,
    pseudo_grad,
    first_moment,
    second_moment,
):
    a, b = {0: cotangent[0]}, {}
    a[-1], a[1] = along_z(a[0], 1), along_z(a[0], -1)
    b[0] = across_x(a[0])

    own = (down_weight[0], gate_weight[0], up_weight[0])
    gate_other = to_sibling(own[1])
    both = [preacts[0], to_sibling(preacts[0])]
    a[-1], a[1], b[0] = after([a[-1], a[1], b[0]], [gate_other, both[1]])
    weights = join(*own, gate_other, to_sibling(pack(own[0], own[2], a[-1])))

    groups = lax.axis_size("group")
    size = groups // 2
    parts = [part.astype(jnp.bfloat16) for part in (pseudo_grad, first_moment, second_moment)]
    fragment = jnp.concatenate(parts, axis=0)
    flips = [[1, 0, 3, 2], [3, 2, 1, 0]]
    swaps = [[(x * size + y, x * size + flip[y]) for x in range(2) for y in range(size)] for flip in flips]
    cots = (a, b)
    a[-2], a[2] = along_z(a[-1], 1), along_z(a[1], -1)
    b[-1], b[1] = across_x(a[-1]), across_x(a[1])
    a[-3], a[3] = along_z(a[-2], 1), along_z(a[2], -1)
    b[-2], b[2] = across_x(a[-2]), across_x(a[2])
    same0, cross0 = chunk_partials(cots, [[(0, 0)], [(1, 0)]], both, weights, [a[-2], a[2]])
    same1, cross1 = chunk_partials(cots, [[(0, 1), (0, -1)], [(1, 1), (1, -1)]], both, weights, [same0])
    a[-3], a[3] = after([a[-3], a[3]], [same1])
    a[4] = along_z(a[-3], 1)
    b[-3], b[3] = across_x(a[-3]), across_x(a[3])
    same2, cross2, cross2_back = chunk_partials(
        cots, [[(0, 2), (0, -2)], [(1, 2)], [(1, -2)]], both, weights, [a[-3], a[3]]
    )
    (fragment,) = after([fragment], [same1])
    paired = add(fragment, lax.ppermute(fragment, "group", swaps[0]))
    (a[4],) = after([a[4]], [same2])
    b[4] = across_x(a[4])
    (same3,) = chunk_partials(cots, [[(0, 3), (0, -3), (0, 4)]], both, weights, [paired])
    (cross3,) = chunk_partials(cots, [[(1, 3), (1, -3)]], both, weights, [same3])
    partners3 = across_x(cross3)

    near, near_back = row_sums(
        ROWS,
        [[(cross1, 0), (along_z(cross2, 1), 0)], [(cross1, ROWS), (along_z(cross2_back, -1), 0)]],
    )
    (cross4,) = chunk_partials(cots, [[(1, 4)]], both, weights, [cross3, near])
    partners4 = across_x(cross4)
    (near0,) = row_sums(ROWS, [[(cross0, 0), (along_z(near, 1), 0), (along_z(near_back, -1), 0)]])
    partners0 = across_x(near0)
    first, second = 0, HALF
    long, long_back = row_sums(
        HALF,
        [[(same3, 2 * ROWS + first), (partners4, first)], [(same3, 2 * ROWS + second), (partners4, second)]],
        [near0, partners3],
    )
    short, short_back = row_sums(
        HALF,
        [[(same3, second), (partners3, second)], [(same3, ROWS + first), (partners3, ROWS + first)]],
    )
    (paired,) = after([paired], [long])
    line = add(paired, lax.ppermute(paired, "group", swaps[1]))
    for held in ([same3, partners3], [same2], [same1]):
        long, long_back = along_z(long, 1), along_z(long_back, -1)
        long, long_back = row_sums(
            HALF,
            [
                [(array, first) for array in held] + [(long, 0)],
                [(array, ROWS + second) for array in held] + [(long_back, 0)],
            ],
            [short] + ([line] if held[0] is same2 else []),
        )
        short, short_back = along_z(short, 1), along_z(short_back, -1)
        if held[0] is not same1:
            ahead = same2 if held[0] is same3 else same1
            short, short_back = row_sums(
                HALF,
                [
                    [(ahead, second), (short, 0)],
                    [(ahead, ROWS + first), (short_back, 0)],
                ],
            )
    long, long_back = along_z(long, 1), along_z(long_back, -1)
    halves = [
        add(same0[:HALF], partners0[:HALF], long, short_back),
        add(same0[HALF:], partners0[HALF:], short, long_back),
    ]
    neighbour = lax.ppermute(line, "group", [(i, (i + size) % groups) for i in range(groups)])
    mean = (line.astype(jnp.float32) + neighbour.astype(jnp.float32)) / groups
    return (jnp.concatenate(halves)[None], mean)


def solution(mesh):
    return jax.shard_map(
        local,
        mesh=mesh,
        in_specs=(
            P("group", "fsdp", None),
            P("group", "fsdp", None),
            P("group", None, "fsdp"),
            P("group", None, "fsdp"),
            P("group", None, None, "fsdp"),
            P("group", "fsdp"),
            P("group", "fsdp"),
            P("group", "fsdp"),
        ),
        out_specs=(P("group", "fsdp", None), P(None, "fsdp")),
        check_vma=False,
    )
```

```python
import functools
import math

import jax
import jax.numpy as jnp
from jax import lax
from jax.experimental import pallas as pl
from jax.experimental.pallas import tpu as pltpu
from jax.sharding import PartitionSpec as P

tanh_scale = math.sqrt(2.0 / math.pi)
cubic_coef = 0.044715

Z, XH, CORE = 8, 2, 2
ROWS = 128
HALF = ROWS // 2
D = 1536
HID = 384
BLOCK = 256
VMEM_BYTES = 24 * 1024 * 1024


def device_of(z, xh, core):
    return ((z % Z) * XH + xh) * CORE + core


def moves(where):
    return [
        (device_of(z, xh, core), device_of(*where(z, xh, core)))
        for z in range(Z)
        for xh in range(XH)
        for core in range(CORE)
    ]


def along_z(value, step):
    return lax.ppermute(value, "fsdp", moves(lambda z, xh, core: (z + step, xh, core)))


def across_x(value):
    return lax.ppermute(value, "fsdp", moves(lambda z, xh, core: (z, 1 - xh, core)))


def to_sibling(value):
    return lax.ppermute(value, "fsdp", moves(lambda z, xh, core: (z, xh, 1 - core)))


def contract_last(left, right):
    return lax.dot_general(left, right, (((1,), (1,)), ((), ())), preferred_element_type=jnp.float32)


ANYWHERE = pl.BlockSpec(memory_space=pl.ANY)
IN_HBM = pl.BlockSpec(memory_space=pltpu.HBM)
ON_CHIP = pl.BlockSpec(memory_space=pltpu.VMEM)
PARAMS = pltpu.CompilerParams(vmem_limit_bytes=VMEM_BYTES)


def move_all(pairs, sems):
    copies = [pltpu.make_async_copy(*pair, sems.at[i]) for i, pair in enumerate(pairs)]
    for copy in copies:
        copy.start()
    return copies


def pack_kernel(down, up, _, packed, sems):
    pairs = [(up, packed.at[pl.ds(0, D), :])]
    for i in range(D // HID):
        pairs.append((down.at[:, pl.ds(i * HID, HID)], packed.at[pl.ds(D + i * HID, HID), :]))
    for copy in move_all(pairs, sems):
        copy.wait()


def pack(down, up, first):
    return pl.pallas_call(
        pack_kernel,
        in_specs=[IN_HBM, IN_HBM, ANYWHERE],
        out_specs=IN_HBM,
        out_shape=jax.ShapeDtypeStruct((2 * D, HID), jnp.bfloat16),
        scratch_shapes=[pltpu.SemaphoreType.DMA((1 + D // HID,))],
        cost_estimate=pl.CostEstimate(flops=0, bytes_accessed=0, transcendentals=0),
        compiler_params=PARAMS,
    )(down, up, first)


def join_kernel(down, gate, up, gate_other, packed, down_both, mixed, sems):
    pairs = [
        (down, down_both.at[pl.ds(0, HID), :]),
        (gate, mixed.at[:, pl.ds(0, HID)]),
        (gate_other, mixed.at[:, pl.ds(HID, HID)]),
        (up, mixed.at[:, pl.ds(2 * HID, HID)]),
        (packed.at[pl.ds(0, D), :], mixed.at[:, pl.ds(3 * HID, HID)]),
    ]
    for i in range(D // HID):
        columns = pl.ds(i * HID, HID)
        pairs.append((packed.at[pl.ds(D + i * HID, HID), :], down_both.at[pl.ds(HID, HID), columns]))
    for copy in move_all(pairs, sems):
        copy.wait()


def join(down, gate, up, gate_other, packed):
    return pl.pallas_call(
        join_kernel,
        in_specs=[IN_HBM] * 3 + [ANYWHERE] * 2,
        out_specs=[ON_CHIP] * 2,
        out_shape=[
            jax.ShapeDtypeStruct((2 * HID, D), jnp.bfloat16),
            jax.ShapeDtypeStruct((D, 4 * HID), jnp.bfloat16),
        ],
        scratch_shapes=[pltpu.SemaphoreType.DMA((5 + D // HID,))],
        cost_estimate=pl.CostEstimate(flops=0, bytes_accessed=0, transcendentals=0),
        compiler_params=PARAMS,
    )(down, gate, up, gate_other, packed)


def grads_kernel(groups, deps, *refs):
    chunks = [chunk for group in groups for chunk in group]
    units = len(chunks)
    cot = refs[:units]
    preacts = refs[units : units + 2]
    down_ref, mixed_ref = refs[units + 2 : units + 4]
    *out_refs, rows_ref, pre_ref, grads_ref, sems = refs[units + 4 + deps :]
    place = lax.axis_index("fsdp")
    core = lax.rem(place, CORE)
    xh = lax.rem(lax.div(place, CORE), XH)
    z = lax.div(place, CORE * XH)
    pairs = []
    for i, (other, k) in enumerate(chunks):
        line = 1 - xh if other else xh
        index = (lax.rem(z + k + Z, Z) * XH + line) * CORE + core
        source = pl.ds(pl.multiple_of(index * ROWS, ROWS), ROWS)
        for j in range(2):
            target = pre_ref.at[:, pl.ds(i * ROWS, ROWS), pl.ds(j * HID, HID)]
            pairs.append((preacts[j].at[:, source, :], target))
    copies = move_all(pairs, sems)
    for i in range(units):
        rows_ref[i * ROWS : (i + 1) * ROWS, :] = cot[i][...]
    for block in range(3):
        left = block * BLOCK
        hidden = contract_last(rows_ref[...], down_ref[left : left + BLOCK, :])
        if block == 0:
            for copy in copies:
                copy.wait()
        for i in range(units):
            rows = slice(i * ROWS, (i + 1) * ROWS)
            gate = pre_ref[0, rows, left : left + BLOCK].astype(jnp.float32)
            up = pre_ref[1, rows, left : left + BLOCK].astype(jnp.float32)
            square = gate * gate
            tanh_part = jnp.tanh(gate * (tanh_scale + (tanh_scale * cubic_coef) * square))
            share = 0.5 + 0.5 * tanh_part
            activated = gate * share
            derivative = share + activated * (1.0 - share) * (
                2.0 * tanh_scale + (6.0 * tanh_scale * cubic_coef) * square
            )
            part = hidden[rows, :]
            grads_ref[rows, left : left + BLOCK] = (part * up * derivative).astype(jnp.bfloat16)
            right = left + 2 * HID
            grads_ref[rows, right : right + BLOCK] = (part * activated).astype(jnp.bfloat16)

    def column_block(step, carry):
        columns = pl.ds(pl.multiple_of(step * BLOCK, BLOCK), BLOCK)
        partial = contract_last(grads_ref[...], mixed_ref[columns, :]).astype(jnp.bfloat16)
        first = 0
        for out_ref in out_refs:
            out_ref[:, columns] = partial[first : first + out_ref.shape[0]]
            first += out_ref.shape[0]
        return carry

    lax.fori_loop(0, D // BLOCK, column_block, 0)


def chunk_partials(cots, groups, preacts, weights, deps=()):
    cot = [cots[other][k] for group in groups for other, k in group]
    units = len(cot)
    rows = units * ROWS
    return pl.pallas_call(
        functools.partial(grads_kernel, groups, len(deps)),
        in_specs=[ON_CHIP] * units + [ANYWHERE] * 2 + [ON_CHIP] * 2 + [ANYWHERE] * len(deps),
        out_specs=[ON_CHIP] * len(groups),
        scratch_shapes=[
            pltpu.VMEM((rows, D), jnp.bfloat16),
            pltpu.VMEM((2, rows, 2 * HID), jnp.bfloat16),
            pltpu.VMEM((rows, 4 * HID), jnp.bfloat16),
            pltpu.SemaphoreType.DMA((2 * units,)),
        ],
        out_shape=[jax.ShapeDtypeStruct((len(group) * ROWS, D), jnp.bfloat16) for group in groups],
        cost_estimate=pl.CostEstimate(
            flops=0,
            bytes_accessed=0,
            transcendentals=0,
        ),
        compiler_params=PARAMS,
    )(*cot, *preacts, *weights, *deps)


def sums_kernel(plan, size, arrays, deps, *refs):
    out_refs = refs[arrays + deps :]
    for out_ref, terms in zip(out_refs, plan):
        total = None
        for array, first in terms:
            term = refs[array][first : first + size, :].astype(jnp.float32)
            total = term if total is None else total + term
        out_ref[...] = total.astype(jnp.bfloat16)


def row_sums(size, plan, deps=()):
    arrays = []
    places = []
    for terms in plan:
        places.append([])
        for array, first in terms:
            if not any(array is known for known in arrays):
                arrays.append(array)
            place = [array is known for known in arrays].index(True)
            places[-1].append((place, first))
    return pl.pallas_call(
        functools.partial(sums_kernel, places, size, len(arrays), len(deps)),
        in_specs=[ON_CHIP] * len(arrays) + [ANYWHERE] * len(deps),
        out_specs=[ON_CHIP] * len(plan),
        out_shape=[jax.ShapeDtypeStruct((size, D), jnp.bfloat16)] * len(plan),
        compiler_params=PARAMS,
    )(*arrays, *deps)


def pass_on(*refs):
    pass


def after(values, first):
    return pl.pallas_call(
        pass_on,
        in_specs=[ANYWHERE] * (len(values) + len(first)),
        out_specs=[ANYWHERE] * len(values),
        out_shape=[jax.ShapeDtypeStruct(value.shape, value.dtype) for value in values],
        input_output_aliases={i: i for i in range(len(values))},
        compiler_params=PARAMS,
    )(*values, *first)


def add(*terms):
    total = terms[0].astype(jnp.float32)
    for term in terms[1:]:
        total = total + term.astype(jnp.float32)
    return total.astype(jnp.bfloat16)


def add(*terms):
    total = terms[0].astype(jnp.float32)
    for term in terms[1:]:
        total = total + term.astype(jnp.float32)
    return total.astype(jnp.bfloat16)


def local(
    cotangent,
    down_weight,
    gate_weight,
    up_weight,
    preacts,
    pseudo_grad,
    first_moment,
    second_moment,
):
    a, b = {0: cotangent[0]}, {}
    a[-1], a[1] = along_z(a[0], 1), along_z(a[0], -1)
    b[0] = across_x(a[0])

    own = (down_weight[0], gate_weight[0], up_weight[0])
    gate_other = to_sibling(own[1])
    both = [preacts[0], to_sibling(preacts[0])]
    a[-1], a[1], b[0] = after([a[-1], a[1], b[0]], [gate_other, both[1]])
    weights = join(*own, gate_other, to_sibling(pack(own[0], own[2], a[-1])))

    groups = lax.axis_size("group")
    size = groups // 2
    parts = [part.astype(jnp.bfloat16) for part in (pseudo_grad, first_moment, second_moment)]
    fragment = jnp.concatenate(parts, axis=0)
    flips = [[1, 0, 3, 2], [3, 2, 1, 0]]
    swaps = [[(x * size + y, x * size + flip[y]) for x in range(2) for y in range(size)] for flip in flips]
    cots = (a, b)
    a[-2], a[2] = along_z(a[-1], 1), along_z(a[1], -1)
    b[1] = across_x(a[1])
    a[-3], a[3] = along_z(a[-2], 1), along_z(a[2], -1)
    b[-2], b[2] = across_x(a[-2]), across_x(a[2])
    same0, cross0 = chunk_partials(cots, [[(0, 0)], [(1, 0)]], both, weights, [a[-2], a[2]])
    (behind,) = after([b[0]], [same0])
    b[-1] = along_z(behind, 1)
    same1, cross1 = chunk_partials(cots, [[(0, 1), (0, -1)], [(1, 1)]], both, weights, [same0])
    a[-3], a[3] = after([a[-3], a[3]], [same1])
    a[4] = along_z(a[-3], 1)
    b[-3], b[3] = across_x(a[-3]), across_x(a[3])
    same2, cross2, cross2_back, cross1_back = chunk_partials(
        cots, [[(0, 2), (0, -2)], [(1, 2)], [(1, -2)], [(1, -1)]], both, weights, [a[-3], a[3]]
    )
    (fragment,) = after([fragment], [same1])
    paired = add(fragment, lax.ppermute(fragment, "group", swaps[0]))
    (a[4],) = after([a[4]], [same2])
    b[4] = across_x(a[4])
    (cross3,) = chunk_partials(cots, [[(1, 3), (1, -3)]], both, weights, [paired])
    partners3 = across_x(cross3)

    near, near_back = row_sums(
        ROWS,
        [[(cross1, 0), (along_z(cross2, 1), 0)], [(cross1_back, 0), (along_z(cross2_back, -1), 0)]],
    )
    (cross4,) = chunk_partials(cots, [[(1, 4)]], both, weights, [cross3, near])
    partners4 = across_x(cross4)
    (same3,) = chunk_partials(cots, [[(0, 3), (0, -3), (0, 4)]], both, weights, [cross4])
    (near0,) = row_sums(ROWS, [[(cross0, 0), (along_z(near, 1), 0), (along_z(near_back, -1), 0)]])
    partners0 = across_x(near0)
    (paired,) = after([paired], [near0])
    line = add(paired, lax.ppermute(paired, "group", swaps[1]))
    first, second = 0, HALF
    long, long_back = row_sums(
        HALF,
        [[(same3, 2 * ROWS + first), (partners4, first)], [(same3, 2 * ROWS + second), (partners4, second)]],
        [near0, partners3],
    )
    short, short_back = row_sums(
        HALF,
        [[(same3, second), (partners3, second)], [(same3, ROWS + first), (partners3, ROWS + first)]],
    )
    for held in ([same3, partners3], [same2], [same1]):
        long, long_back = along_z(long, 1), along_z(long_back, -1)
        long, long_back = row_sums(
            HALF,
            [
                [(array, first) for array in held] + [(long, 0)],
                [(array, ROWS + second) for array in held] + [(long_back, 0)],
            ],
            [short] + ([line] if held[0] is same3 else []),
        )
        short, short_back = along_z(short, 1), along_z(short_back, -1)
        if held[0] is not same1:
            ahead = same2 if held[0] is same3 else same1
            short, short_back = row_sums(
                HALF,
                [
                    [(ahead, second), (short, 0)],
                    [(ahead, ROWS + first), (short_back, 0)],
                ],
            )
    long, long_back = along_z(long, 1), along_z(long_back, -1)
    halves = [
        add(same0[:HALF], partners0[:HALF], long, short_back),
        add(same0[HALF:], partners0[HALF:], short, long_back),
    ]
    neighbour = lax.ppermute(line, "group", [(i, (i + size) % groups) for i in range(groups)])
    mean = (line.astype(jnp.float32) + neighbour.astype(jnp.float32)) / groups
    return (jnp.concatenate(halves)[None], mean)


def solution(mesh):
    return jax.shard_map(
        local,
        mesh=mesh,
        in_specs=(
            P("group", "fsdp", None),
            P("group", "fsdp", None),
            P("group", None, "fsdp"),
            P("group", None, "fsdp"),
            P("group", None, None, "fsdp"),
            P("group", "fsdp"),
            P("group", "fsdp"),
            P("group", "fsdp"),
        ),
        out_specs=(P("group", "fsdp", None), P(None, "fsdp")),
        check_vma=False,
    )
```

```python
import functools
import math

import jax
import jax.numpy as jnp
from jax import lax
from jax.experimental import pallas as pl
from jax.experimental.pallas import tpu as pltpu
from jax.sharding import PartitionSpec as P

tanh_scale = math.sqrt(2.0 / math.pi)
cubic_coef = 0.044715

Z, XH, CORE = 8, 2, 2
ROWS = 128
HALF = ROWS // 2
D = 1536
HID = 384
BLOCK = 256
VMEM_BYTES = 24 * 1024 * 1024


def device_of(z, xh, core):
    return ((z % Z) * XH + xh) * CORE + core


def moves(where):
    return [
        (device_of(z, xh, core), device_of(*where(z, xh, core)))
        for z in range(Z)
        for xh in range(XH)
        for core in range(CORE)
    ]


def along_z(value, step):
    return lax.ppermute(value, "fsdp", moves(lambda z, xh, core: (z + step, xh, core)))


def across_x(value):
    return lax.ppermute(value, "fsdp", moves(lambda z, xh, core: (z, 1 - xh, core)))


def to_sibling(value):
    return lax.ppermute(value, "fsdp", moves(lambda z, xh, core: (z, xh, 1 - core)))


def contract_last(left, right):
    return lax.dot_general(left, right, (((1,), (1,)), ((), ())), preferred_element_type=jnp.float32)


ANYWHERE = pl.BlockSpec(memory_space=pl.ANY)
IN_HBM = pl.BlockSpec(memory_space=pltpu.HBM)
ON_CHIP = pl.BlockSpec(memory_space=pltpu.VMEM)
PARAMS = pltpu.CompilerParams(vmem_limit_bytes=VMEM_BYTES)


def move_all(pairs, sems):
    copies = [pltpu.make_async_copy(*pair, sems.at[i]) for i, pair in enumerate(pairs)]
    for copy in copies:
        copy.start()
    return copies


def pack_kernel(down, up, _, packed, sems):
    pairs = [(up, packed.at[pl.ds(0, D), :])]
    for i in range(D // HID):
        pairs.append((down.at[:, pl.ds(i * HID, HID)], packed.at[pl.ds(D + i * HID, HID), :]))
    for copy in move_all(pairs, sems):
        copy.wait()


def pack(down, up, first):
    return pl.pallas_call(
        pack_kernel,
        in_specs=[IN_HBM, IN_HBM, ANYWHERE],
        out_specs=IN_HBM,
        out_shape=jax.ShapeDtypeStruct((2 * D, HID), jnp.bfloat16),
        scratch_shapes=[pltpu.SemaphoreType.DMA((1 + D // HID,))],
        cost_estimate=pl.CostEstimate(flops=0, bytes_accessed=0, transcendentals=0),
        compiler_params=PARAMS,
    )(down, up, first)


def join_kernel(down, gate, up, gate_other, packed, down_both, mixed, sems):
    pairs = [
        (down, down_both.at[pl.ds(0, HID), :]),
        (gate, mixed.at[:, pl.ds(0, HID)]),
        (gate_other, mixed.at[:, pl.ds(HID, HID)]),
        (up, mixed.at[:, pl.ds(2 * HID, HID)]),
        (packed.at[pl.ds(0, D), :], mixed.at[:, pl.ds(3 * HID, HID)]),
    ]
    for i in range(D // HID):
        columns = pl.ds(i * HID, HID)
        pairs.append((packed.at[pl.ds(D + i * HID, HID), :], down_both.at[pl.ds(HID, HID), columns]))
    for copy in move_all(pairs, sems):
        copy.wait()


def join(down, gate, up, gate_other, packed):
    return pl.pallas_call(
        join_kernel,
        in_specs=[IN_HBM] * 3 + [ANYWHERE] * 2,
        out_specs=[ON_CHIP] * 2,
        out_shape=[
            jax.ShapeDtypeStruct((2 * HID, D), jnp.bfloat16),
            jax.ShapeDtypeStruct((D, 4 * HID), jnp.bfloat16),
        ],
        scratch_shapes=[pltpu.SemaphoreType.DMA((5 + D // HID,))],
        cost_estimate=pl.CostEstimate(flops=0, bytes_accessed=0, transcendentals=0),
        compiler_params=PARAMS,
    )(down, gate, up, gate_other, packed)


def grads_kernel(groups, deps, *refs):
    chunks = [chunk for group in groups for chunk in group]
    units = len(chunks)
    cot = refs[:units]
    preacts = refs[units : units + 2]
    down_ref, mixed_ref = refs[units + 2 : units + 4]
    *out_refs, rows_ref, pre_ref, grads_ref, sems = refs[units + 4 + deps :]
    place = lax.axis_index("fsdp")
    core = lax.rem(place, CORE)
    xh = lax.rem(lax.div(place, CORE), XH)
    z = lax.div(place, CORE * XH)
    pairs = []
    for i, (other, k) in enumerate(chunks):
        line = 1 - xh if other else xh
        index = (lax.rem(z + k + Z, Z) * XH + line) * CORE + core
        source = pl.ds(pl.multiple_of(index * ROWS, ROWS), ROWS)
        for j in range(2):
            target = pre_ref.at[:, pl.ds(i * ROWS, ROWS), pl.ds(j * HID, HID)]
            pairs.append((preacts[j].at[:, source, :], target))
    copies = move_all(pairs, sems)
    for i in range(units):
        rows_ref[i * ROWS : (i + 1) * ROWS, :] = cot[i][...]
    for block in range(3):
        left = block * BLOCK
        hidden = contract_last(rows_ref[...], down_ref[left : left + BLOCK, :])
        if block == 0:
            for copy in copies:
                copy.wait()
        for i in range(units):
            rows = slice(i * ROWS, (i + 1) * ROWS)
            gate = pre_ref[0, rows, left : left + BLOCK].astype(jnp.float32)
            up = pre_ref[1, rows, left : left + BLOCK].astype(jnp.float32)
            square = gate * gate
            tanh_part = jnp.tanh(gate * (tanh_scale + (tanh_scale * cubic_coef) * square))
            share = 0.5 + 0.5 * tanh_part
            activated = gate * share
            derivative = share + activated * (1.0 - share) * (
                2.0 * tanh_scale + (6.0 * tanh_scale * cubic_coef) * square
            )
            part = hidden[rows, :]
            grads_ref[rows, left : left + BLOCK] = (part * up * derivative).astype(jnp.bfloat16)
            right = left + 2 * HID
            grads_ref[rows, right : right + BLOCK] = (part * activated).astype(jnp.bfloat16)

    def column_block(step, carry):
        columns = pl.ds(pl.multiple_of(step * BLOCK, BLOCK), BLOCK)
        partial = contract_last(grads_ref[...], mixed_ref[columns, :]).astype(jnp.bfloat16)
        first = 0
        for out_ref in out_refs:
            out_ref[:, columns] = partial[first : first + out_ref.shape[0]]
            first += out_ref.shape[0]
        return carry

    lax.fori_loop(0, D // BLOCK, column_block, 0)


def chunk_partials(cots, groups, preacts, weights, deps=()):
    cot = [cots[other][k] for group in groups for other, k in group]
    units = len(cot)
    rows = units * ROWS
    return pl.pallas_call(
        functools.partial(grads_kernel, groups, len(deps)),
        in_specs=[ON_CHIP] * units + [ANYWHERE] * 2 + [ON_CHIP] * 2 + [ANYWHERE] * len(deps),
        out_specs=[ON_CHIP] * len(groups),
        scratch_shapes=[
            pltpu.VMEM((rows, D), jnp.bfloat16),
            pltpu.VMEM((2, rows, 2 * HID), jnp.bfloat16),
            pltpu.VMEM((rows, 4 * HID), jnp.bfloat16),
            pltpu.SemaphoreType.DMA((2 * units,)),
        ],
        out_shape=[jax.ShapeDtypeStruct((len(group) * ROWS, D), jnp.bfloat16) for group in groups],
        cost_estimate=pl.CostEstimate(
            flops=0,
            bytes_accessed=0,
            transcendentals=0,
        ),
        compiler_params=PARAMS,
    )(*cot, *preacts, *weights, *deps)


def sums_kernel(plan, size, arrays, deps, *refs):
    out_refs = refs[arrays + deps :]
    for out_ref, terms in zip(out_refs, plan):
        total = None
        for array, first in terms:
            term = refs[array][first : first + size, :].astype(jnp.float32)
            total = term if total is None else total + term
        out_ref[...] = total.astype(jnp.bfloat16)


def row_sums(size, plan, deps=()):
    arrays = []
    places = []
    for terms in plan:
        places.append([])
        for array, first in terms:
            if not any(array is known for known in arrays):
                arrays.append(array)
            place = [array is known for known in arrays].index(True)
            places[-1].append((place, first))
    return pl.pallas_call(
        functools.partial(sums_kernel, places, size, len(arrays), len(deps)),
        in_specs=[ON_CHIP] * len(arrays) + [ANYWHERE] * len(deps),
        out_specs=[ON_CHIP] * len(plan),
        out_shape=[jax.ShapeDtypeStruct((size, D), jnp.bfloat16)] * len(plan),
        compiler_params=PARAMS,
    )(*arrays, *deps)


def pass_on(*refs):
    pass


def after(values, first):
    return pl.pallas_call(
        pass_on,
        in_specs=[ANYWHERE] * (len(values) + len(first)),
        out_specs=[ANYWHERE] * len(values),
        out_shape=[jax.ShapeDtypeStruct(value.shape, value.dtype) for value in values],
        input_output_aliases={i: i for i in range(len(values))},
        compiler_params=PARAMS,
    )(*values, *first)


def add(*terms):
    total = terms[0].astype(jnp.float32)
    for term in terms[1:]:
        total = total + term.astype(jnp.float32)
    return total.astype(jnp.bfloat16)


def add(*terms):
    total = terms[0].astype(jnp.float32)
    for term in terms[1:]:
        total = total + term.astype(jnp.float32)
    return total.astype(jnp.bfloat16)


def local(
    cotangent,
    down_weight,
    gate_weight,
    up_weight,
    preacts,
    pseudo_grad,
    first_moment,
    second_moment,
):
    a, b = {0: cotangent[0]}, {}
    a[-1], a[1] = along_z(a[0], 1), along_z(a[0], -1)
    b[0] = across_x(a[0])

    own = (down_weight[0], gate_weight[0], up_weight[0])
    gate_other = to_sibling(own[1])
    both = [preacts[0], to_sibling(preacts[0])]
    a[-1], a[1] = after([a[-1], a[1]], [gate_other, both[1]])
    weights = join(*own, gate_other, to_sibling(pack(own[0], own[2], a[-1])))

    groups = lax.axis_size("group")
    size = groups // 2
    parts = [part.astype(jnp.bfloat16) for part in (pseudo_grad, first_moment, second_moment)]
    fragment = jnp.concatenate(parts, axis=0)
    flips = [[1, 0, 3, 2], [3, 2, 1, 0]]
    swaps = [[(x * size + y, x * size + flip[y]) for x in range(2) for y in range(size)] for flip in flips]
    cots = (a, b)
    a[-2], a[2] = along_z(a[-1], 1), along_z(a[1], -1)
    b[1] = across_x(a[1])
    a[-3], a[3] = along_z(a[-2], 1), along_z(a[2], -1)
    b[-2], b[2] = across_x(a[-2]), across_x(a[2])
    same0, cross0 = chunk_partials(cots, [[(0, 0)], [(1, 0)]], both, weights, [a[-2], a[2]])
    (fragment,) = after([fragment], [a[-1]])
    paired = add(fragment, lax.ppermute(fragment, "group", swaps[0]))
    (behind,) = after([b[0]], [same0])
    b[-1] = along_z(behind, 1)
    same1, cross1 = chunk_partials(cots, [[(0, 1), (0, -1)], [(1, 1)]], both, weights, [same0, paired])
    a[-3], a[3] = after([a[-3], a[3]], [same1])
    a[4] = along_z(a[-3], 1)
    b[-3], b[3] = across_x(a[-3]), across_x(a[3])
    same2, cross2, cross2_back, cross1_back = chunk_partials(
        cots, [[(0, 2), (0, -2)], [(1, 2)], [(1, -2)], [(1, -1)]], both, weights, [a[-3], a[3]]
    )
    (a[4],) = after([a[4]], [same2])
    b[4] = across_x(a[4])
    (cross3,) = chunk_partials(cots, [[(1, 3), (1, -3)]], both, weights)
    partners3 = across_x(cross3)

    cross2, cross2_back = along_z(cross2, 1), along_z(cross2_back, -1)
    (same3,) = chunk_partials(cots, [[(0, 3), (0, -3), (0, 4)]], both, weights, [cross3])
    (cross4,) = chunk_partials(cots, [[(1, 4)]], both, weights, [same3, cross2, cross2_back])
    partners4 = across_x(cross4)
    near, near_back = row_sums(
        ROWS, [[(cross1, 0), (cross2, 0)], [(cross1_back, 0), (cross2_back, 0)]], [cross4]
    )
    (near0,) = row_sums(ROWS, [[(cross0, 0), (along_z(near, 1), 0), (along_z(near_back, -1), 0)]])
    partners0 = across_x(near0)
    (paired,) = after([paired], [near0])
    line = add(paired, lax.ppermute(paired, "group", swaps[1]))
    first, second = 0, HALF
    long, long_back = row_sums(
        HALF,
        [[(same3, 2 * ROWS + first), (partners4, first)], [(same3, 2 * ROWS + second), (partners4, second)]],
        [partners3],
    )
    short, short_back = row_sums(
        HALF,
        [[(same3, second), (partners3, second)], [(same3, ROWS + first), (partners3, ROWS + first)]],
    )
    for held in ([same3, partners3], [same2], [same1]):
        long, long_back = along_z(long, 1), along_z(long_back, -1)
        long, long_back = row_sums(
            HALF,
            [
                [(array, first) for array in held] + [(long, 0)],
                [(array, ROWS + second) for array in held] + [(long_back, 0)],
            ],
            [short] + ([near0] if held[0] is same3 else [line] if held[0] is same2 else []),
        )
        short, short_back = along_z(short, 1), along_z(short_back, -1)
        if held[0] is not same1:
            ahead = same2 if held[0] is same3 else same1
            short, short_back = row_sums(
                HALF,
                [
                    [(ahead, second), (short, 0)],
                    [(ahead, ROWS + first), (short_back, 0)],
                ],
            )
    long, long_back = along_z(long, 1), along_z(long_back, -1)
    halves = [
        add(same0[:HALF], partners0[:HALF], long, short_back),
        add(same0[HALF:], partners0[HALF:], short, long_back),
    ]
    neighbour = lax.ppermute(line, "group", [(i, (i + size) % groups) for i in range(groups)])
    mean = (line.astype(jnp.float32) + neighbour.astype(jnp.float32)) / groups
    return (jnp.concatenate(halves)[None], mean)


def solution(mesh):
    return jax.shard_map(
        local,
        mesh=mesh,
        in_specs=(
            P("group", "fsdp", None),
            P("group", "fsdp", None),
            P("group", None, "fsdp"),
            P("group", None, "fsdp"),
            P("group", None, None, "fsdp"),
            P("group", "fsdp"),
            P("group", "fsdp"),
            P("group", "fsdp"),
        ),
        out_specs=(P("group", "fsdp", None), P(None, "fsdp")),
        check_vma=False,
    )
```

```python
import functools
import math

import jax
import jax.numpy as jnp
from jax import lax
from jax.experimental import pallas as pl
from jax.experimental.pallas import tpu as pltpu
from jax.sharding import PartitionSpec as P

tanh_scale = math.sqrt(2.0 / math.pi)
cubic_coef = 0.044715

Z, XH, CORE = 8, 2, 2
ROWS = 128
HALF = ROWS // 2
D = 1536
HID = 384
BLOCK = 256
VMEM_BYTES = 24 * 1024 * 1024


def device_of(z, xh, core):
    return ((z % Z) * XH + xh) * CORE + core


def moves(where):
    return [
        (device_of(z, xh, core), device_of(*where(z, xh, core)))
        for z in range(Z)
        for xh in range(XH)
        for core in range(CORE)
    ]


def along_z(value, step):
    return lax.ppermute(value, "fsdp", moves(lambda z, xh, core: (z + step, xh, core)))


def across_x(value):
    return lax.ppermute(value, "fsdp", moves(lambda z, xh, core: (z, 1 - xh, core)))


def to_sibling(value):
    return lax.ppermute(value, "fsdp", moves(lambda z, xh, core: (z, xh, 1 - core)))


def contract_last(left, right):
    return lax.dot_general(left, right, (((1,), (1,)), ((), ())), preferred_element_type=jnp.float32)


ANYWHERE = pl.BlockSpec(memory_space=pl.ANY)
IN_HBM = pl.BlockSpec(memory_space=pltpu.HBM)
ON_CHIP = pl.BlockSpec(memory_space=pltpu.VMEM)
PARAMS = pltpu.CompilerParams(vmem_limit_bytes=VMEM_BYTES)


def move_all(pairs, sems):
    copies = [pltpu.make_async_copy(*pair, sems.at[i]) for i, pair in enumerate(pairs)]
    for copy in copies:
        copy.start()
    return copies


def pack_kernel(down, up, _, packed, sems):
    pairs = [(up, packed.at[pl.ds(0, D), :])]
    for i in range(D // HID):
        pairs.append((down.at[:, pl.ds(i * HID, HID)], packed.at[pl.ds(D + i * HID, HID), :]))
    for copy in move_all(pairs, sems):
        copy.wait()


def pack(down, up, first):
    return pl.pallas_call(
        pack_kernel,
        in_specs=[IN_HBM, IN_HBM, ANYWHERE],
        out_specs=IN_HBM,
        out_shape=jax.ShapeDtypeStruct((2 * D, HID), jnp.bfloat16),
        scratch_shapes=[pltpu.SemaphoreType.DMA((1 + D // HID,))],
        cost_estimate=pl.CostEstimate(flops=0, bytes_accessed=0, transcendentals=0),
        compiler_params=PARAMS,
    )(down, up, first)


def join_kernel(down, gate, up, gate_other, packed, down_both, mixed, sems):
    pairs = [
        (down, down_both.at[pl.ds(0, HID), :]),
        (gate, mixed.at[:, pl.ds(0, HID)]),
        (gate_other, mixed.at[:, pl.ds(HID, HID)]),
        (up, mixed.at[:, pl.ds(2 * HID, HID)]),
        (packed.at[pl.ds(0, D), :], mixed.at[:, pl.ds(3 * HID, HID)]),
    ]
    for i in range(D // HID):
        columns = pl.ds(i * HID, HID)
        pairs.append((packed.at[pl.ds(D + i * HID, HID), :], down_both.at[pl.ds(HID, HID), columns]))
    for copy in move_all(pairs, sems):
        copy.wait()


def join(down, gate, up, gate_other, packed):
    return pl.pallas_call(
        join_kernel,
        in_specs=[IN_HBM] * 3 + [ANYWHERE] * 2,
        out_specs=[ON_CHIP] * 2,
        out_shape=[
            jax.ShapeDtypeStruct((2 * HID, D), jnp.bfloat16),
            jax.ShapeDtypeStruct((D, 4 * HID), jnp.bfloat16),
        ],
        scratch_shapes=[pltpu.SemaphoreType.DMA((5 + D // HID,))],
        cost_estimate=pl.CostEstimate(flops=0, bytes_accessed=0, transcendentals=0),
        compiler_params=PARAMS,
    )(down, gate, up, gate_other, packed)


def grads_kernel(groups, deps, *refs):
    chunks = [chunk for group in groups for chunk in group]
    units = len(chunks)
    cot = refs[:units]
    preacts = refs[units : units + 2]
    down_ref, mixed_ref = refs[units + 2 : units + 4]
    *out_refs, rows_ref, pre_ref, grads_ref, sems = refs[units + 4 + deps :]
    place = lax.axis_index("fsdp")
    core = lax.rem(place, CORE)
    xh = lax.rem(lax.div(place, CORE), XH)
    z = lax.div(place, CORE * XH)
    pairs = []
    for i, (other, k) in enumerate(chunks):
        line = 1 - xh if other else xh
        index = (lax.rem(z + k + Z, Z) * XH + line) * CORE + core
        source = pl.ds(pl.multiple_of(index * ROWS, ROWS), ROWS)
        for j in range(2):
            target = pre_ref.at[:, pl.ds(i * ROWS, ROWS), pl.ds(j * HID, HID)]
            pairs.append((preacts[j].at[:, source, :], target))
    copies = move_all(pairs, sems)
    for i in range(units):
        rows_ref[i * ROWS : (i + 1) * ROWS, :] = cot[i][...]
    for block in range(3):
        left = block * BLOCK
        hidden = contract_last(rows_ref[...], down_ref[left : left + BLOCK, :])
        if block == 0:
            for copy in copies:
                copy.wait()
        for i in range(units):
            rows = slice(i * ROWS, (i + 1) * ROWS)
            gate = pre_ref[0, rows, left : left + BLOCK].astype(jnp.float32)
            up = pre_ref[1, rows, left : left + BLOCK].astype(jnp.float32)
            square = gate * gate
            tanh_part = jnp.tanh(gate * (tanh_scale + (tanh_scale * cubic_coef) * square))
            share = 0.5 + 0.5 * tanh_part
            activated = gate * share
            derivative = share + activated * (1.0 - share) * (
                2.0 * tanh_scale + (6.0 * tanh_scale * cubic_coef) * square
            )
            part = hidden[rows, :]
            grads_ref[rows, left : left + BLOCK] = (part * up * derivative).astype(jnp.bfloat16)
            right = left + 2 * HID
            grads_ref[rows, right : right + BLOCK] = (part * activated).astype(jnp.bfloat16)

    def column_block(step, carry):
        columns = pl.ds(pl.multiple_of(step * BLOCK, BLOCK), BLOCK)
        partial = contract_last(grads_ref[...], mixed_ref[columns, :]).astype(jnp.bfloat16)
        first = 0
        for out_ref in out_refs:
            out_ref[:, columns] = partial[first : first + out_ref.shape[0]]
            first += out_ref.shape[0]
        return carry

    lax.fori_loop(0, D // BLOCK, column_block, 0)


def chunk_partials(cots, groups, preacts, weights, deps=()):
    cot = [cots[other][k] for group in groups for other, k in group]
    units = len(cot)
    rows = units * ROWS
    return pl.pallas_call(
        functools.partial(grads_kernel, groups, len(deps)),
        in_specs=[ON_CHIP] * units + [ANYWHERE] * 2 + [ON_CHIP] * 2 + [ANYWHERE] * len(deps),
        out_specs=[ON_CHIP] * len(groups),
        scratch_shapes=[
            pltpu.VMEM((rows, D), jnp.bfloat16),
            pltpu.VMEM((2, rows, 2 * HID), jnp.bfloat16),
            pltpu.VMEM((rows, 4 * HID), jnp.bfloat16),
            pltpu.SemaphoreType.DMA((2 * units,)),
        ],
        out_shape=[jax.ShapeDtypeStruct((len(group) * ROWS, D), jnp.bfloat16) for group in groups],
        cost_estimate=pl.CostEstimate(
            flops=0,
            bytes_accessed=0,
            transcendentals=0,
        ),
        compiler_params=PARAMS,
    )(*cot, *preacts, *weights, *deps)


def sums_kernel(plan, size, arrays, deps, *refs):
    out_refs = refs[arrays + deps :]
    for out_ref, terms in zip(out_refs, plan):
        total = None
        for array, first in terms:
            term = refs[array][first : first + size, :].astype(jnp.float32)
            total = term if total is None else total + term
        out_ref[...] = total.astype(jnp.bfloat16)


def row_sums(size, plan, deps=()):
    arrays = []
    places = []
    for terms in plan:
        places.append([])
        for array, first in terms:
            if not any(array is known for known in arrays):
                arrays.append(array)
            place = [array is known for known in arrays].index(True)
            places[-1].append((place, first))
    return pl.pallas_call(
        functools.partial(sums_kernel, places, size, len(arrays), len(deps)),
        in_specs=[ON_CHIP] * len(arrays) + [ANYWHERE] * len(deps),
        out_specs=[ON_CHIP] * len(plan),
        out_shape=[jax.ShapeDtypeStruct((size, D), jnp.bfloat16)] * len(plan),
        compiler_params=PARAMS,
    )(*arrays, *deps)


def final_kernel(same, crossed, long, short_back, short, long_back, out, total, sems):
    copies = []
    for i, (left, right) in enumerate(((long, short_back), (short, long_back))):
        rows = pl.ds(i * HALF, HALF)
        terms = [ref[rows, :].astype(jnp.float32) for ref in (same, crossed)]
        terms += [ref[...].astype(jnp.float32) for ref in (left, right)]
        total[rows, :] = (terms[0] + terms[1] + terms[2] + terms[3]).astype(jnp.bfloat16)
        copies.append(pltpu.make_async_copy(total.at[rows, :], out.at[rows, :], sems.at[i]))
        copies[-1].start()
    for copy in copies:
        copy.wait()


def final_sum(*arrays):
    return pl.pallas_call(
        final_kernel,
        in_specs=[ON_CHIP] * 6,
        out_specs=IN_HBM,
        out_shape=jax.ShapeDtypeStruct((ROWS, D), jnp.bfloat16),
        scratch_shapes=[pltpu.VMEM((ROWS, D), jnp.bfloat16), pltpu.SemaphoreType.DMA((2,))],
        compiler_params=PARAMS,
    )(*arrays)


def pass_on(*refs):
    pass


def after(values, first):
    return pl.pallas_call(
        pass_on,
        in_specs=[ANYWHERE] * (len(values) + len(first)),
        out_specs=[ANYWHERE] * len(values),
        out_shape=[jax.ShapeDtypeStruct(value.shape, value.dtype) for value in values],
        input_output_aliases={i: i for i in range(len(values))},
        compiler_params=PARAMS,
    )(*values, *first)


def add(*terms):
    total = terms[0].astype(jnp.float32)
    for term in terms[1:]:
        total = total + term.astype(jnp.float32)
    return total.astype(jnp.bfloat16)


def add(*terms):
    total = terms[0].astype(jnp.float32)
    for term in terms[1:]:
        total = total + term.astype(jnp.float32)
    return total.astype(jnp.bfloat16)


def local(
    cotangent,
    down_weight,
    gate_weight,
    up_weight,
    preacts,
    pseudo_grad,
    first_moment,
    second_moment,
):
    a, b = {0: cotangent[0]}, {}
    a[-1], a[1] = along_z(a[0], 1), along_z(a[0], -1)
    b[0] = across_x(a[0])

    own = (down_weight[0], gate_weight[0], up_weight[0])
    gate_other = to_sibling(own[1])
    both = [preacts[0], to_sibling(preacts[0])]
    a[-1], a[1], b[0] = after([a[-1], a[1], b[0]], [gate_other, both[1]])
    weights = join(*own, gate_other, to_sibling(pack(own[0], own[2], a[-1])))

    groups = lax.axis_size("group")
    size = groups // 2
    parts = [part.astype(jnp.bfloat16) for part in (pseudo_grad, first_moment, second_moment)]
    fragment = jnp.concatenate(parts, axis=0)
    flips = [[1, 0, 3, 2], [3, 2, 1, 0]]
    swaps = [[(x * size + y, x * size + flip[y]) for x in range(2) for y in range(size)] for flip in flips]
    cots = (a, b)
    a[-2], a[2] = along_z(a[-1], 1), along_z(a[1], -1)
    b[1] = across_x(a[1])
    a[-3], a[3] = along_z(a[-2], 1), along_z(a[2], -1)
    b[-2], b[2] = across_x(a[-2]), across_x(a[2])
    same0, cross0 = chunk_partials(cots, [[(0, 0)], [(1, 0)]], both, weights, [a[-2], a[2]])
    (behind,) = after([b[0]], [same0])
    b[-1] = along_z(behind, 1)
    same1, cross1 = chunk_partials(cots, [[(0, 1), (0, -1)], [(1, 1)]], both, weights, [same0])
    a[-3], a[3] = after([a[-3], a[3]], [same1])
    a[4] = along_z(a[-3], 1)
    b[-3], b[3] = across_x(a[-3]), across_x(a[3])
    same2, cross2, cross2_back, cross1_back = chunk_partials(
        cots, [[(0, 2), (0, -2)], [(1, 2)], [(1, -2)], [(1, -1)]], both, weights, [a[-3], a[3]]
    )
    (fragment,) = after([fragment], [same1])
    paired = add(fragment, lax.ppermute(fragment, "group", swaps[0]))
    (a[4],) = after([a[4]], [same2])
    b[4] = across_x(a[4])
    (cross3,) = chunk_partials(cots, [[(1, 3), (1, -3)]], both, weights, [paired])
    partners3 = across_x(cross3)

    near, near_back = row_sums(
        ROWS,
        [[(cross1, 0), (along_z(cross2, 1), 0)], [(cross1_back, 0), (along_z(cross2_back, -1), 0)]],
    )
    (cross4,) = chunk_partials(cots, [[(1, 4)]], both, weights, [cross3, near])
    partners4 = across_x(cross4)
    (same3,) = chunk_partials(cots, [[(0, 3), (0, -3), (0, 4)]], both, weights, [cross4])
    (near0,) = row_sums(ROWS, [[(cross0, 0), (along_z(near, 1), 0), (along_z(near_back, -1), 0)]])
    partners0 = across_x(near0)
    (paired,) = after([paired], [near0])
    line = add(paired, lax.ppermute(paired, "group", swaps[1]))
    first, second = 0, HALF
    long, long_back = row_sums(
        HALF,
        [[(same3, 2 * ROWS + first), (partners4, first)], [(same3, 2 * ROWS + second), (partners4, second)]],
        [near0, partners3],
    )
    short, short_back = row_sums(
        HALF,
        [[(same3, second), (partners3, second)], [(same3, ROWS + first), (partners3, ROWS + first)]],
    )
    for held in ([same3, partners3], [same2], [same1]):
        long, long_back = along_z(long, 1), along_z(long_back, -1)
        long, long_back = row_sums(
            HALF,
            [
                [(array, first) for array in held] + [(long, 0)],
                [(array, ROWS + second) for array in held] + [(long_back, 0)],
            ],
            [short] + ([line] if held[0] is same3 else []),
        )
        short, short_back = along_z(short, 1), along_z(short_back, -1)
        if held[0] is not same1:
            ahead = same2 if held[0] is same3 else same1
            short, short_back = row_sums(
                HALF,
                [
                    [(ahead, second), (short, 0)],
                    [(ahead, ROWS + first), (short_back, 0)],
                ],
            )
    long, long_back = along_z(long, 1), along_z(long_back, -1)
    summed = final_sum(same0, partners0, long, short_back, short, long_back)
    neighbour = lax.ppermute(line, "group", [(i, (i + size) % groups) for i in range(groups)])
    mean = (line.astype(jnp.float32) + neighbour.astype(jnp.float32)) / groups
    return (summed[None], mean)


def solution(mesh):
    return jax.shard_map(
        local,
        mesh=mesh,
        in_specs=(
            P("group", "fsdp", None),
            P("group", "fsdp", None),
            P("group", None, "fsdp"),
            P("group", None, "fsdp"),
            P("group", None, None, "fsdp"),
            P("group", "fsdp"),
            P("group", "fsdp"),
            P("group", "fsdp"),
        ),
        out_specs=(P("group", "fsdp", None), P(None, "fsdp")),
        check_vma=False,
    )
```
